32 devices in a mesh: bins: 8 (over y, x, core), slab: 4 (over z).
Axes of the slice: x: 2, y: 2, z: 4, core: 2. Of those that a mesh axis runs over, the one named last changes fastest.
Arguments:
- free_velocity: float32 [6, 262144], P(None, ('bins', 'slab')), may hold values from -9 to 9
- inverse_mass: float32 [6, 262144], P(None, ('bins', 'slab')), may hold values from 0.5 to 2
- first_body: int32 [131072], P(('bins', 'slab')), may hold values from 0 to 8191
- second_body: int32 [131072], P(('bins', 'slab')), may hold values from 0 to 20479
- send_list: int32 [8, 49152], P(None, ('bins', 'slab')), may hold values from 0 to 8191
- jacobian: float32 [2, 3, 6, 131072], P(None, None, None, ('bins', 'slab')), may hold values from -2.5 to 2.5
- contact_bias: float32 [3, 131072], P(None, ('bins', 'slab')), may hold values from -27 to 27
- compliance: float32 [131072], P(('bins', 'slab')), may hold values from 0.05 to 0.5
- friction: float32 [131072], P(('bins', 'slab')), may hold values from 0.2 to 0.9
- warm_start: float32 [3, 131072], P(None, ('bins', 'slab')), may hold values from -4.5 to 4.5
Outputs:
- impulses: float32 [3, 131072], P(None, ('bins', 'slab'))
- velocity: float32 [6, 262144], P(None, ('bins', 'slab'))
The draws below stay inside these ranges and needn't reach their ends.
All inputs are finite; a program needn't handle non-finite values.
Results may differ from the reference program's by a relative error of at most 0.0003.
Values sent between devices are 32-bit elements; how exact they have to be, the bound alone decides.
A program may use at most 128 MiB of HBM per device.

```python
import math
import jax
import jax.numpy as jnp

B_DEV = 8192
C_DEV = 4096
HALO_CAP = 1536
ITERS = 3
BODIES = 262144
CONTACTS = 131072
SENDS = 49152
N_BINS = 8
N_SLAB = 4


def bins_ramp(total_count, per_device):
    device = jnp.arange(total_count) // per_device
    bin_row = device // N_SLAB
    return 1.0 + 2.0 * bin_row.astype(jnp.float32) / max(N_BINS - 1, 1)


def draw_second_body(key, part):
    key = jax.random.fold_in(key, 11)
    subkeys = jax.random.split(key, 4)
    positions = jnp.arange(CONTACTS, dtype=jnp.int32)
    device = positions // C_DEV
    bin_row = device // N_SLAB
    slab_column = device % N_SLAB
    remote_draw = jax.random.randint(subkeys[0], (CONTACTS,), 0, 4)
    direction_code = jax.random.randint(subkeys[1], (CONTACTS,), 0, 12)
    face_table = jnp.array([1, 3, 4, 6], dtype=jnp.int32)
    direction = jnp.where(direction_code < 8, direction_code, face_table[jnp.clip(direction_code - 8, 0, 3)])
    row_table = jnp.array([-1, -1, -1, 0, 0, 1, 1, 1], dtype=jnp.int32)
    column_table = jnp.array([-1, 0, 1, -1, 1, -1, 0, 1], dtype=jnp.int32)
    target_row = bin_row + row_table[direction]
    target_column = slab_column + column_table[direction]
    exists = (target_row >= 0) & (target_row < N_BINS) & (target_column >= 0) & (target_column < N_SLAB)
    halo_slot = jax.random.randint(subkeys[2], (CONTACTS,), 0, HALO_CAP)
    local_body = jax.random.randint(subkeys[3], (CONTACTS,), 0, B_DEV)
    remote_value = B_DEV + direction * HALO_CAP + halo_slot
    return jnp.where((remote_draw == 0) & exists, remote_value, local_body).astype(jnp.int32)


def draw_contact_bias(key, part):
    key = jax.random.fold_in(key, 21)
    subkeys = jax.random.split(key, 2)
    ramp = bins_ramp(CONTACTS, C_DEV)
    spread = jnp.exp(jax.random.uniform(subkeys[1], (1, CONTACTS), minval=math.log(0.3), maxval=math.log(3.0)))
    values = jnp.clip(jax.random.normal(subkeys[0], (3, CONTACTS)), -3.0, 3.0)
    return (ramp * spread * values).astype(jnp.float32)


def draw_warm_start(key, part):
    key = jax.random.fold_in(key, 31)
    ramp = bins_ramp(CONTACTS, C_DEV)
    values = jnp.clip(jax.random.normal(key, (3, CONTACTS)), -3.0, 3.0)
    return (0.5 * ramp * values).astype(jnp.float32)


def draw_free_velocity(key, part):
    key = jax.random.fold_in(key, 41)
    ramp = bins_ramp(BODIES, B_DEV)
    values = jnp.clip(jax.random.normal(key, (6, BODIES)), -3.0, 3.0)
    return (ramp * values).astype(jnp.float32)


def set_ends(values, stream_key, least, top_value):
    extent = values.shape
    spot = [jax.random.randint(jax.random.fold_in(stream_key, axis), (), 0, extent[axis]) for axis in range(len(extent))]
    values = values.at[tuple(spot)].set(least)
    longest = extent.index(max(extent))
    spot[longest] = (spot[longest] + 1) % extent[longest]
    return values.at[tuple(spot)].set(top_value)


def block_levels(stream_key, extent, shards, least, high):
    factor_of, own = 1.0, jax.random.fold_in(stream_key, 6)
    for axis_at, blocks in shards:
        draws = jnp.exp(jax.random.uniform(jax.random.fold_in(own, axis_at), (blocks,), jnp.float32, least / len(shards), high / len(shards)))
        factor_of = factor_of * jnp.repeat(draws, extent[axis_at] // blocks).reshape([-1 if axis == axis_at else 1 for axis in range(len(extent))])
    return factor_of


def scatter_about(rng, shape, deviation, bound, shards=(), kind=jnp.bfloat16):
    values = jax.random.normal(rng, shape, jnp.float32) * deviation
    if len(shards) > 0:
        values = block_levels(rng, shape, shards, -0.22, 0.18) * values
    return jnp.clip(values, min=-bound, max=bound).astype(kind)


def setup_inputs(seed: int = 0) -> dict:
    keys = jax.random.split(jax.random.key(seed), 11)
    return {
        "free_velocity": draw_free_velocity(jax.random.fold_in(keys[10], 71), 0),
        "inverse_mass": jnp.clip(jnp.exp(math.log(2.0) - 1.3862944 * jax.random.uniform(keys[1], (6, BODIES), jnp.float32) ** block_levels(keys[1], (6, BODIES), ((1, 32),), -0.2, 0.2)), 0.5, 2.0),
        "first_body": set_ends(jax.random.randint(keys[2], (CONTACTS,), 0, B_DEV), jax.random.fold_in(keys[2], 1), 0, B_DEV - 1).astype(jnp.int32),
        "second_body": draw_second_body(jax.random.fold_in(keys[10], 71), 0),
        "send_list": set_ends(jax.random.randint(keys[4], (8, SENDS), 0, B_DEV), jax.random.fold_in(keys[4], 1), 0, B_DEV - 1).astype(jnp.int32),
        "jacobian": scatter_about(keys[5], (2, 3, 6, CONTACTS), 6 ** -0.5, 2.5, ((3, 32),), jnp.float32),
        "contact_bias": draw_contact_bias(jax.random.fold_in(keys[10], 71), 0),
        "compliance": jnp.clip(jnp.exp(math.log(0.5) - 2.3025851 * jax.random.uniform(keys[7], (CONTACTS,), jnp.float32) ** block_levels(keys[7], (CONTACTS,), ((0, 32),), -0.2, 0.2)), 0.05, 0.5),
        "friction": jnp.clip(0.2 + 0.7 * jax.random.uniform(keys[8], (CONTACTS,), jnp.float32) ** block_levels(keys[8], (CONTACTS,), ((0, 32),), -0.2, 0.2), 0.2, 0.9),
        "warm_start": draw_warm_start(jax.random.fold_in(keys[10], 71), 0),
    }


bin_steps = (-1, -1, -1, 0, 0, 1, 1, 1)
slab_steps = (-1, 0, 1, -1, 1, -1, 0, 1)
SAFETY = 0.3
TINY = 1e-06
FLOOR = 1e-20

def momentum_table(steps_count):
    theta_now = 1.0
    momentum = []
    for iteration in range(steps_count):
        theta_next = (-theta_now * theta_now + theta_now * math.sqrt(theta_now * theta_now + 4.0)) / 2.0
        momentum.append(theta_now * (1.0 - theta_now) / (theta_now * theta_now + theta_next))
        theta_now = theta_next
    return momentum

def project(values, friction):
    normal = values[0]
    tangent_one = values[1]
    tangent_two = values[2]
    magnitude = jnp.sqrt(tangent_one * tangent_one + tangent_two * tangent_two)
    projected = jnp.maximum(friction * magnitude + normal, 0.0) / (friction * friction + 1.0)
    inside = magnitude <= friction * normal
    normal_new = jnp.where(inside, normal, projected)
    tangent_limit = friction * normal_new
    factor = tangent_limit / jnp.maximum(jnp.maximum(magnitude, tangent_limit), FLOOR)
    return jnp.stack([normal_new, tangent_one * factor, tangent_two * factor])

def reference(free_velocity, inverse_mass, first_body, second_body, send_list, jacobian, contact_bias, compliance, friction, warm_start):
    positions = jnp.arange(CONTACTS, dtype=jnp.int32)
    device = positions // C_DEV
    bin_row = device // N_SLAB
    slab_column = device % N_SLAB
    first_global = device * B_DEV + first_body
    is_local = second_body < B_DEV
    halo_index = jnp.maximum(second_body - B_DEV, 0)
    direction = jnp.minimum(halo_index // HALO_CAP, 7)
    halo_slot = halo_index % HALO_CAP
    row_table = jnp.array(bin_steps, dtype=jnp.int32)
    column_table = jnp.array(slab_steps, dtype=jnp.int32)
    source_row = jnp.clip(bin_row + row_table[direction], 0, N_BINS - 1)
    source_column = jnp.clip(slab_column + column_table[direction], 0, N_SLAB - 1)
    source = source_row * N_SLAB + source_column
    remote_body = send_list[7 - direction, source * HALO_CAP + halo_slot]
    second_global = jnp.where(is_local, device * B_DEV + second_body, source * B_DEV + remote_body)
    first_blocks = jacobian[0]
    second_blocks = jacobian[1]

    def spread(multipliers):
        first_terms = first_blocks[0] * multipliers[0] + first_blocks[1] * multipliers[1] + first_blocks[2] * multipliers[2]
        second_terms = second_blocks[0] * multipliers[0] + second_blocks[1] * multipliers[1] + second_blocks[2] * multipliers[2]
        accumulator = jnp.zeros((6, BODIES), jnp.float32)
        accumulator = accumulator.at[:, first_global].add(first_terms)
        return accumulator.at[:, second_global].add(second_terms)

    def gradient(velocity, multipliers):
        first_speed = velocity[:, first_global]
        second_speed = velocity[:, second_global]
        result = contact_bias + compliance * multipliers
        for column in range(6):
            result = result + first_blocks[:, column] * first_speed[column] + second_blocks[:, column] * second_speed[column]
        return result
    momentum = momentum_table(ITERS)
    contacts_total = 3.0 * CONTACTS
    previous_point = jnp.zeros_like(warm_start)
    previous_forces = jnp.zeros((6, BODIES), jnp.float32)
    impulses = warm_start
    extrapolated = warm_start
    for iteration in range(ITERS):
        current = spread(extrapolated)
        change = extrapolated - previous_point
        force_change = current - previous_forces
        total_squares = jnp.sum(change * change)
        total_curve = jnp.sum(inverse_mass * force_change * force_change) + jnp.sum(compliance * change * change)
        stepsize = SAFETY * (total_squares / contacts_total + TINY) / (total_curve / contacts_total + TINY)
        velocity = free_velocity + inverse_mass * current
        gradient_now = gradient(velocity, extrapolated)
        updated = project(extrapolated - stepsize * gradient_now, friction)
        previous_point = extrapolated
        previous_forces = current
        extrapolated = updated + momentum[iteration] * (updated - impulses)
        impulses = updated
    final_forces = spread(impulses)
    return (impulses, free_velocity + inverse_mass * final_forces)
```

```python
import functools
import math

import jax
import jax.numpy as jnp
from jax import lax
from jax.experimental import pallas as pl
from jax.experimental.pallas import tpu as pltpu
from jax.sharding import PartitionSpec as P

ITERS = 3
SAFETY = 0.3
TINY = 1e-06
FLOOR = 1e-20
HI = 256
BF = jnp.bfloat16
F32 = jnp.float32
MESH = pl.DeviceIdType.MESH


def momentum_table(steps_count):
    theta_now = 1.0
    momentum = []
    for iteration in range(steps_count):
        theta_next = (
            -theta_now * theta_now + theta_now * math.sqrt(theta_now * theta_now + 4.0)
        ) / 2.0
        momentum.append(theta_now * (1.0 - theta_now) / (theta_now * theta_now + theta_next))
        theta_now = theta_next
    return momentum


def project(normal, tangent_one, tangent_two, friction):
    magnitude = jnp.sqrt(tangent_one * tangent_one + tangent_two * tangent_two)
    projected = jnp.maximum(friction * magnitude + normal, 0.0) / (friction * friction + 1.0)
    inside = magnitude <= friction * normal
    normal_new = jnp.where(inside, normal, projected)
    tangent_limit = friction * normal_new
    factor = tangent_limit / jnp.maximum(jnp.maximum(magnitude, tangent_limit), FLOOR)
    return normal_new, tangent_one * factor, tangent_two * factor


def split_rows(values):
    lead = values.astype(BF).astype(F32)
    return jnp.concatenate([lead, values - lead], axis=-2).astype(BF)


def chunk(index, width):
    return pl.ds(pl.multiple_of(index * width, width), width)


def kernel(
    n_bins, n_slab,
    fv_ref, im_ref, first_ref, second_ref, list_ref, jac_ref, bias_ref, comp_ref, fric_ref, warm_ref,
    imp_ref, vel_ref,
    hot, lo32, lo16, halo_hot, halo_lo32, halo_lo16,
    fvb, imb, x8, x16, acc, acc_halo, force, force_old, av, speed,
    point, point_old, gamma,
    out_f, out_v, in_f, in_v, part, sum_one, sum_two,
    send_f, recv_f, send_v, recv_v, send_one, recv_one, send_two, recv_two,
):
    bodies = fv_ref.shape[1]
    contacts = first_ref.shape[1]
    halo = list_ref.shape[1]
    n_lo = bodies // HI
    h_lo = halo // HI
    halo_los = 8 * h_lo
    ck = 512
    contacts_total = 3.0 * contacts * n_bins * n_slab
    b = lax.axis_index("bins")
    s = lax.axis_index("slab")

    def place(e):
        g = e + (e + 4) // 8
        return b + g // 3 - 1, s + g % 3 - 1

    def exists(e):
        nb, ns = place(e)
        return (nb >= 0) & (nb < n_bins) & (ns >= 0) & (ns < n_slab)

    def loop(count, body):
        def step(i, carry):
            body(i)
            return carry
        lax.fori_loop(0, count, step, 0)

    in_f[...] = jnp.zeros_like(in_f)
    in_v[...] = jnp.zeros_like(in_v)

    barrier = pltpu.get_barrier_semaphore()

    @functools.partial(loop, 8)
    def greet(e):
        @pl.when(exists(e))
        def _():
            pl.semaphore_signal(barrier, inc=1, device_id=place(e), device_id_type=MESH)

    @functools.partial(loop, n_slab - 1)
    def greet_slab(i):
        pl.semaphore_signal(barrier, inc=1, device_id=(b, (s + 1 + i) % n_slab), device_id_type=MESH)

    @functools.partial(loop, n_bins - 1)
    def greet_bins(i):
        pl.semaphore_signal(barrier, inc=1, device_id=((b + 1 + i) % n_bins, s), device_id_type=MESH)

    rows = lax.broadcasted_iota(jnp.int32, (HI, ck), 0)

    def index_parts(index, hot_to, lo32_to, lo16_to):
        low = jnp.broadcast_to(index // HI, (16, ck))
        hot_to[...] = jnp.where(rows == index % HI, 1.0, 0.0).astype(BF)
        lo32_to[...] = low[:8]
        lo16_to[...] = low.astype(F32).astype(BF)

    @functools.partial(loop, contacts // ck)
    def prepare(i):
        for half, ref in enumerate((first_ref, second_ref)):
            to = pl.ds(pl.multiple_of(half * contacts + i * ck, ck), ck)
            index_parts(ref[:, chunk(i, ck)], hot.at[:, to], lo32.at[:, to], lo16.at[:, to])

    for e in range(8):
        for c in range(halo // ck):
            to = pl.ds(c * ck, ck)
            index_parts(
                list_ref[e:e + 1, to],
                halo_hot.at[e, :, to], halo_lo32.at[e, :, to], halo_lo16.at[e, :, to],
            )

    fvb[...] = jnp.zeros_like(fvb)
    imb[...] = jnp.zeros_like(imb)
    for l in range(n_lo):
        fvb[l, 0:6, :] = fv_ref[:, l * HI:(l + 1) * HI]
        imb[l, 0:6, :] = im_ref[:, l * HI:(l + 1) * HI]
    x8[...] = jnp.zeros_like(x8)
    force_old[...] = jnp.zeros_like(force_old)
    point_old[...] = jnp.zeros_like(point_old)
    point[...] = warm_ref[...]
    gamma[...] = warm_ref[...]

    others = (n_slab - 1) + (n_bins - 1)
    up = jnp.where(b < n_bins - 1, 1, 0)
    down = jnp.where(b > 0, 1, 0)
    right = jnp.where(s < n_slab - 1, 1, 0)
    left = jnp.where(s > 0, 1, 0)
    pl.semaphore_wait(barrier, (1 + up + down) * (1 + left + right) - 1 + others)

    def copy(source, target, send, recv, e):
        return pltpu.make_async_remote_copy(
            src_ref=source.at[e], dst_ref=target.at[7 - e],
            send_sem=send.at[e], recv_sem=recv.at[7 - e],
            device_id=place(e), device_id_type=MESH,
        )

    def arrival(source, target, send, recv, e):
        return pltpu.make_async_remote_copy(
            src_ref=source.at[e], dst_ref=target.at[e],
            send_sem=send.at[e], recv_sem=recv.at[e],
            device_id=place(e), device_id_type=MESH,
        )

    def scatter(values, low, hot_part, first_lo, count):
        zero = jnp.zeros_like(values)
        tall = jnp.concatenate(
            [jnp.where(low == jnp.array(first_lo + l, BF), values, zero) for l in range(count)], axis=0
        )
        return lax.dot_general(tall, hot_part, (((1,), (1,)), ((), ())), preferred_element_type=F32)

    def gather(table, low, hot_part, first_lo, count):
        picked = jnp.dot(table, hot_part, preferred_element_type=F32)
        total = None
        for l in range(count):
            both = picked[l * 16:l * 16 + 8] + picked[l * 16 + 8:l * 16 + 16]
            both = jnp.where(low == first_lo + l, both, 0.0)
            total = both if total is None else total + both
        return total

    def spread(source):
        @functools.partial(loop, contacts // ck)
        def terms(i):
            at = chunk(i, ck)
            for half in range(2):
                x8[half, 0:6, :] = (
                    jac_ref[half, 0, :, at] * source[0:1, at]
                    + jac_ref[half, 1, :, at] * source[1:2, at]
                    + jac_ref[half, 2, :, at] * source[2:3, at]
                )
                x16[:, pl.ds(pl.multiple_of(half * contacts + i * ck, ck), ck)] = split_rows(x8[half])

        acc_halo[...] = jnp.zeros_like(acc_halo)

        @functools.partial(loop, contacts // ck)
        def halo_part(i):
            at = pl.ds(pl.multiple_of(contacts + i * ck, ck), ck)
            acc_halo[...] += scatter(x16[:, at], lo16[:, at], hot[:, at], n_lo, halo_los)

        for e in range(8):
            for m in range(h_lo):
                row = (e * h_lo + m) * 16
                out_f[e, :, m * HI:(m + 1) * HI] = acc_halo[row:row + 8] + acc_halo[row + 8:row + 16]

        @functools.partial(loop, 8)
        def send(e):
            @pl.when(exists(e))
            def _():
                copy(out_f, in_f, send_f, recv_f, e).start()

        acc[...] = jnp.zeros_like(acc)

        @functools.partial(loop, 2 * contacts // ck)
        def local_part(i):
            at = chunk(i, ck)
            acc[...] += scatter(x16[:, at], lo16[:, at], hot[:, at], 0, n_lo)

        @functools.partial(loop, 8)
        def arrived(e):
            @pl.when(exists(e))
            def _():
                arrival(out_f, in_f, send_f, recv_f, e).wait_recv()
            for c in range(halo // ck):
                at = pl.ds(c * ck, ck)
                acc[...] += scatter(
                    split_rows(in_f[e, :, at]), halo_lo16[e, :, at], halo_hot[e, :, at], 0, n_lo
                )

        both = acc[...].reshape(n_lo, 2, 8, HI)
        force[...] = both[:, 0] + both[:, 1]

        @functools.partial(loop, 8)
        def sent(e):
            @pl.when(exists(e))
            def _():
                copy(out_f, in_f, send_f, recv_f, e).wait_send()

    def lanes(values):
        row = jnp.sum(values, axis=0, keepdims=True)
        total = row[:, 0:128]
        for c in range(1, row.shape[1] // 128):
            total = total + row[:, c * 128:(c + 1) * 128]
        return total

    def slab_copy(k, i, slot):
        other = (s + 1 + i) % n_slab
        at = s if slot is None else slot
        return pltpu.make_async_remote_copy(
            src_ref=part.at[0], dst_ref=sum_one.at[k, at],
            send_sem=send_one.at[i], recv_sem=recv_one.at[k, at],
            device_id=(b, other), device_id_type=MESH,
        )

    def bins_copy(k, i, slot):
        other = (b + 1 + i) % n_bins
        at = b if slot is None else slot
        return pltpu.make_async_remote_copy(
            src_ref=part.at[1], dst_ref=sum_two.at[k, at],
            send_sem=send_two.at[i], recv_sem=recv_two.at[k, at],
            device_id=(other, s), device_id_type=MESH,
        )

    momentum = momentum_table(ITERS)

    def iteration(k):
        spread(point)

        change = point[...] - point_old[...]
        squares = change * change
        shift = force[...] - force_old[...]
        curve = (imb[...] * shift * shift).reshape(n_lo * 8, HI)
        part[0, 0:1, :] = lanes(squares)
        part[0, 1:2, :] = lanes(curve) + lanes(comp_ref[...] * squares)
        part[0, 2:8, :] = jnp.zeros((6, 128), F32)

        @functools.partial(loop, n_slab - 1)
        def send_slab(i):
            slab_copy(k, i, None).start()
        sum_one[k, s] = part[0]

        velocity = fvb[...] + imb[...] * force[...]
        av[0:n_lo * 16, :] = split_rows(velocity).reshape(n_lo * 16, HI)

        @functools.partial(loop, 8)
        def pull(e):
            for c in range(halo // ck):
                at = pl.ds(c * ck, ck)
                out_v[e, :, at] = gather(
                    av[0:n_lo * 16, :], halo_lo32[e, :, at], halo_hot[e, :, at], 0, n_lo
                )

            @pl.when(exists(e))
            def _():
                copy(out_v, in_v, send_v, recv_v, e).start()

        @functools.partial(loop, n_slab - 1)
        def wait_slab(i):
            slab_copy(k, i, (s + 1 + i) % n_slab).wait_recv()
        part[1] = functools.reduce(lambda x, y: x + y, [sum_one[k, i] for i in range(n_slab)])

        @functools.partial(loop, n_bins - 1)
        def send_bins(i):
            bins_copy(k, i, None).start()
        sum_two[k, b] = part[1]

        @functools.partial(loop, 2 * contacts // ck)
        def local_part(i):
            at = chunk(i, ck)
            speed[:, at] = gather(av[0:n_lo * 16, :], lo32[:, at], hot[:, at], 0, n_lo)

        @functools.partial(loop, n_bins - 1)
        def wait_bins(i):
            bins_copy(k, i, (b + 1 + i) % n_bins).wait_recv()
        total = functools.reduce(lambda x, y: x + y, [sum_two[k, i] for i in range(n_bins)])
        total = jnp.sum(total, axis=1, keepdims=True)
        step = (
            SAFETY * (total[0:1] / contacts_total + TINY) / (total[1:2] / contacts_total + TINY)
        )

        @functools.partial(loop, 8)
        def arrived(e):
            @pl.when(exists(e))
            def _():
                arrival(out_v, in_v, send_v, recv_v, e).wait_recv()
            for m in range(h_lo):
                row = pl.multiple_of((n_lo + e * h_lo + m) * 16, 16)
                av[pl.ds(row, 16), :] = split_rows(in_v[e, :, m * HI:(m + 1) * HI])

        beta = jnp.where(k == 0, momentum[0], jnp.where(k == 1, momentum[1], momentum[2])).astype(F32)

        @functools.partial(loop, contacts // ck)
        def update(i):
            at = chunk(i, ck)
            to = pl.ds(pl.multiple_of(contacts + i * ck, ck), ck)
            second = speed[:, to] + gather(
                av[n_lo * 16:, :], lo32[:, to], hot[:, to], n_lo, halo_los
            )
            second = second[0:6]
            first = speed[0:6, at]
            compliance = comp_ref[:, at]
            moved = []
            for r in range(3):
                here = point[r:r + 1, at]
                product = jac_ref[0, r, :, at] * first + jac_ref[1, r, :, at] * second
                slope = bias_ref[r:r + 1, at] + compliance * here + jnp.sum(product, axis=0, keepdims=True)
                moved.append(here - step * slope)
            updated = project(*moved, fric_ref[:, at])
            for r in range(3):
                point_old[r:r + 1, at] = point[r:r + 1, at]
                point[r:r + 1, at] = updated[r] + beta * (updated[r] - gamma[r:r + 1, at])
                gamma[r:r + 1, at] = updated[r]

        force_old[...] = force[...]

        @functools.partial(loop, 8)
        def sent(e):
            @pl.when(exists(e))
            def _():
                copy(out_v, in_v, send_v, recv_v, e).wait_send()

        @functools.partial(loop, n_slab - 1)
        def sent_slab(i):
            slab_copy(k, i, None).wait_send()

        @functools.partial(loop, n_bins - 1)
        def sent_bins(i):
            bins_copy(k, i, None).wait_send()

    loop(ITERS, iteration)
    spread(gamma)
    imp_ref[...] = gamma[...]
    for l in range(n_lo):
        vel_ref[:, l * HI:(l + 1) * HI] = (fvb[l] + imb[l] * force[l])[0:6]


def shards(
    n_bins, n_slab,
    free_velocity, inverse_mass, first_body, second_body, send_list,
    jacobian, contact_bias, compliance, friction, warm_start,
):
    bodies = free_velocity.shape[1]
    contacts = first_body.shape[0]
    halo = send_list.shape[1]
    n_lo = bodies // HI
    all_lo = n_lo + 8 * (halo // HI)
    dma = pltpu.SemaphoreType.DMA
    vm = pltpu.VMEM
    scratch = [
        vm((HI, 2 * contacts), BF), vm((8, 2 * contacts), jnp.int32), vm((16, 2 * contacts), BF),
        vm((8, HI, halo), BF), vm((8, 8, halo), jnp.int32), vm((8, 16, halo), BF),
        vm((n_lo, 8, HI), F32), vm((n_lo, 8, HI), F32), vm((2, 8, 512), F32), vm((16, 2 * contacts), BF),
        vm((n_lo * 16, HI), F32), vm(((all_lo - n_lo) * 16, HI), F32),
        vm((n_lo, 8, HI), F32), vm((n_lo, 8, HI), F32), vm((all_lo * 16, HI), BF), vm((8, 2 * contacts), F32),
        vm((3, contacts), F32), vm((3, contacts), F32), vm((3, contacts), F32),
        vm((8, 8, halo), F32), vm((8, 8, halo), F32), vm((8, 8, halo), F32), vm((8, 8, halo), F32),
        vm((2, 8, 128), F32), vm((ITERS, n_slab, 8, 128), F32), vm((ITERS, n_bins, 8, 128), F32),
        dma((8,)), dma((8,)), dma((8,)), dma((8,)),
        dma((n_slab,)), dma((ITERS, n_slab)), dma((n_bins,)), dma((ITERS, n_bins)),
    ]
    spec = pl.BlockSpec(memory_space=pltpu.VMEM)
    return pl.pallas_call(
        functools.partial(kernel, n_bins, n_slab),
        out_shape=(
            jax.ShapeDtypeStruct((3, contacts), F32),
            jax.ShapeDtypeStruct((6, bodies), F32),
        ),
        in_specs=[spec] * 10,
        out_specs=(spec, spec),
        scratch_shapes=scratch,
        compiler_params=pltpu.CompilerParams(
            collective_id=0, has_side_effects=True, vmem_limit_bytes=48 * 1024 * 1024
        ),
    )(
        free_velocity, inverse_mass, first_body[None], second_body[None], send_list,
        jacobian, contact_bias, compliance[None], friction[None], warm_start,
    )


def solution(mesh):
    return jax.shard_map(
        functools.partial(shards, mesh.shape["bins"], mesh.shape["slab"]),
        mesh=mesh,
        in_specs=(
            P(None, ("bins", "slab")),
            P(None, ("bins", "slab")),
            P(("bins", "slab")),
            P(("bins", "slab")),
            P(None, ("bins", "slab")),
            P(None, None, None, ("bins", "slab")),
            P(None, ("bins", "slab")),
            P(("bins", "slab")),
            P(("bins", "slab")),
            P(None, ("bins", "slab")),
        ),
        out_specs=(P(None, ("bins", "slab")), P(None, ("bins", "slab"))),
        check_vma=False,
    )
```

```python
import functools
import math

import jax
import jax.numpy as jnp
from jax import lax
from jax.experimental import pallas as pl
from jax.experimental.pallas import tpu as pltpu
from jax.sharding import PartitionSpec as P

ITERS = 3
SAFETY = 0.3
TINY = 1e-06
FLOOR = 1e-20
HI = 256
BF = jnp.bfloat16
F32 = jnp.float32
MESH = pl.DeviceIdType.MESH


def momentum_table(steps_count):
    theta_now = 1.0
    momentum = []
    for iteration in range(steps_count):
        theta_next = (
            -theta_now * theta_now + theta_now * math.sqrt(theta_now * theta_now + 4.0)
        ) / 2.0
        momentum.append(theta_now * (1.0 - theta_now) / (theta_now * theta_now + theta_next))
        theta_now = theta_next
    return momentum


def project(normal, tangent_one, tangent_two, friction):
    magnitude = jnp.sqrt(tangent_one * tangent_one + tangent_two * tangent_two)
    projected = jnp.maximum(friction * magnitude + normal, 0.0) / (friction * friction + 1.0)
    inside = magnitude <= friction * normal
    normal_new = jnp.where(inside, normal, projected)
    tangent_limit = friction * normal_new
    factor = tangent_limit / jnp.maximum(jnp.maximum(magnitude, tangent_limit), FLOOR)
    return normal_new, tangent_one * factor, tangent_two * factor


def split(values):
    lead = values.astype(BF).astype(F32)
    return lead, values - lead


def pack(values):
    lead, rest = split(values)
    twice = jnp.concatenate([lead, rest, lead, rest], axis=0)
    return jnp.concatenate([twice, twice], axis=0).astype(BF)


def chunk(index, width):
    return pl.ds(pl.multiple_of(index * width, width), width)


def kernel(
    n_bins, n_slab,
    fv_ref, im_ref, first_ref, second_ref, list_ref, jac_ref, bias_ref, comp_ref, fric_ref, warm_ref,
    imp_ref, vel_ref,
    hot, lo32, lo16, halo_hot, halo_lo32, halo_lo16,
    fvb, imb, x48, acc, acc_halo, force, force_old, table, av, speed,
    point, point_old, gamma,
    out_f, out_v, in_f, in_v, part, sum_one, sum_two,
    send_f, recv_f, send_v, recv_v, send_one, recv_one, send_two, recv_two,
):
    bodies = fv_ref.shape[1]
    contacts = first_ref.shape[1]
    halo = list_ref.shape[1]
    n_lo = bodies // HI
    h_lo = halo // HI
    halo_los = 8 * h_lo
    ck = 512
    contacts_total = 3.0 * contacts * n_bins * n_slab
    b = lax.axis_index("bins")
    s = lax.axis_index("slab")

    def place(e):
        g = e + (e + 4) // 8
        return b + g // 3 - 1, s + g % 3 - 1

    def exists(e):
        nb, ns = place(e)
        return (nb >= 0) & (nb < n_bins) & (ns >= 0) & (ns < n_slab)

    def loop(count, body):
        def step(i, carry):
            body(i)
            return carry
        lax.fori_loop(0, count, step, 0)

    in_f[...] = jnp.zeros_like(in_f)
    in_v[...] = jnp.zeros_like(in_v)

    barrier = pltpu.get_barrier_semaphore()

    @functools.partial(loop, 8)
    def greet(e):
        @pl.when(exists(e))
        def _():
            pl.semaphore_signal(barrier, inc=1, device_id=place(e), device_id_type=MESH)

    @functools.partial(loop, n_slab - 1)
    def greet_slab(i):
        pl.semaphore_signal(barrier, inc=1, device_id=(b, (s + 1 + i) % n_slab), device_id_type=MESH)

    @functools.partial(loop, n_bins - 1)
    def greet_bins(i):
        pl.semaphore_signal(barrier, inc=1, device_id=((b + 1 + i) % n_bins, s), device_id_type=MESH)

    rows = lax.broadcasted_iota(jnp.int32, (HI, ck), 0)

    def index_parts(index, hot_to, lo32_to, lo16_to):
        low = jnp.broadcast_to(index // HI, (16, ck))
        hot_to[...] = jnp.where(rows == index % HI, 1.0, 0.0).astype(BF)
        lo32_to[...] = low[:8]
        lo16_to[...] = low.astype(F32).astype(BF)

    @functools.partial(loop, contacts // ck)
    def prepare(i):
        for half, ref in enumerate((first_ref, second_ref)):
            to = pl.ds(pl.multiple_of(half * contacts + i * ck, ck), ck)
            index_parts(ref[:, chunk(i, ck)], hot.at[:, to], lo32.at[:, to], lo16.at[:, to])

    def prepare_halo():
        for e in range(8):
            for c in range(halo // ck):
                to = pl.ds(c * ck, ck)
                index_parts(
                    list_ref[e:e + 1, to],
                    halo_hot.at[e, :, to], halo_lo32.at[e, :, to], halo_lo16.at[e, :, to],
                )
        for l in range(n_lo):
            fvb[l, 0:6, :] = fv_ref[:, l * HI:(l + 1) * HI]
            imb[l, 0:6, :] = im_ref[:, l * HI:(l + 1) * HI]

    fvb[...] = jnp.zeros_like(fvb)
    imb[...] = jnp.zeros_like(imb)
    out_f[...] = jnp.zeros_like(out_f)
    out_v[...] = jnp.zeros_like(out_v)
    force[...] = jnp.zeros_like(force)
    force_old[...] = jnp.zeros_like(force_old)
    point_old[...] = jnp.zeros_like(point_old)
    point[...] = warm_ref[...]
    gamma[...] = warm_ref[...]

    others = (n_slab - 1) + (n_bins - 1)
    up = jnp.where(b < n_bins - 1, 1, 0)
    down = jnp.where(b > 0, 1, 0)
    right = jnp.where(s < n_slab - 1, 1, 0)
    left = jnp.where(s > 0, 1, 0)
    pl.semaphore_wait(barrier, (1 + up + down) * (1 + left + right) - 1 + others)

    def copy(source, target, send, recv, e):
        return pltpu.make_async_remote_copy(
            src_ref=source.at[e], dst_ref=target.at[7 - e],
            send_sem=send.at[e], recv_sem=recv.at[7 - e],
            device_id=place(e), device_id_type=MESH,
        )

    def arrival(source, target, send, recv, e):
        return pltpu.make_async_remote_copy(
            src_ref=source.at[e], dst_ref=target.at[e],
            send_sem=send.at[e], recv_sem=recv.at[e],
            device_id=place(e), device_id_type=MESH,
        )

    def scatter(values, low, hot_part, first_lo, count):
        tiles = [None] * (count * 12 // 16)
        zero = jnp.zeros(low.shape, BF)
        for t in range(3):
            owner = (lax.broadcasted_iota(jnp.int32, low.shape, 0) + 16 * t) // 12
            left_over = low - owner.astype(F32).astype(BF)
            part_t = values[16 * t:16 * t + 16]
            for j in range(count // 4):
                tiles[3 * j + t] = jnp.where(left_over == jnp.array(first_lo + 4 * j, BF), part_t, zero)
        tall = jnp.concatenate(tiles, axis=0)
        return lax.dot_general(tall, hot_part, (((1,), (1,)), ((), ())), preferred_element_type=F32)

    def gather(rows_of, low, hot_part, first_lo, count):
        picked = jnp.dot(rows_of, hot_part, preferred_element_type=F32)
        sums = []
        for t in range(3):
            left_over = low - (lax.broadcasted_iota(jnp.int32, low.shape, 0) + 8 * t) // 12
            total = None
            for j in range(count // 2):
                row = (3 * j + t) * 8
                term = jnp.where(left_over == first_lo + 2 * j, picked[row:row + 8], 0.0)
                total = term if total is None else total + term
            sums.append(total)
        sums = jnp.concatenate(sums, axis=0)
        return (sums[0:6] + sums[6:12]) + (sums[12:18] + sums[18:24])

    def spread(meanwhile=None):
        @functools.partial(loop, contacts // ck)
        def terms(i):
            at = chunk(i, ck)
            for half in range(2):
                x48[:, pl.ds(pl.multiple_of(half * contacts + i * ck, ck), ck)] = pack(
                    jac_ref[half, 0, :, at] * point[0:1, at]
                    + jac_ref[half, 1, :, at] * point[1:2, at]
                    + jac_ref[half, 2, :, at] * point[2:3, at]
                )

        acc_halo[...] = jnp.zeros_like(acc_halo)

        @functools.partial(loop, contacts // ck)
        def halo_part(i):
            at = pl.ds(pl.multiple_of(contacts + i * ck, ck), ck)
            acc_halo[...] += scatter(x48[:, at], lo16[:, at], hot[:, at], n_lo, halo_los)

        for e in range(8):
            for m in range(h_lo):
                row = (e * h_lo + m) * 12
                out_f[e, 0:6, m * HI:(m + 1) * HI] = acc_halo[row:row + 6] + acc_halo[row + 6:row + 12]

        @functools.partial(loop, 8)
        def send(e):
            @pl.when(exists(e))
            def _():
                copy(out_f, in_f, send_f, recv_f, e).start()

        if meanwhile is not None:
            meanwhile()
        acc[...] = jnp.zeros_like(acc)

        @functools.partial(loop, 2 * contacts // ck)
        def local_part(i):
            at = chunk(i, ck)
            acc[...] += scatter(x48[:, at], lo16[:, at], hot[:, at], 0, n_lo)

        @functools.partial(loop, 8)
        def arrived(e):
            @pl.when(exists(e))
            def _():
                arrival(out_f, in_f, send_f, recv_f, e).wait_recv()
            for c in range(halo // ck):
                at = pl.ds(c * ck, ck)
                acc[...] += scatter(
                    pack(in_f[e, 0:6, at]), halo_lo16[e, :, at], halo_hot[e, :, at], 0, n_lo
                )

        for l in range(n_lo):
            force[l, 0:6, :] = acc[l * 12:l * 12 + 6] + acc[l * 12 + 6:l * 12 + 12]

        @functools.partial(loop, 8)
        def sent(e):
            @pl.when(exists(e))
            def _():
                copy(out_f, in_f, send_f, recv_f, e).wait_send()

    def lanes(values):
        row = jnp.sum(values, axis=0, keepdims=True)
        total = row[:, 0:128]
        for c in range(1, row.shape[1] // 128):
            total = total + row[:, c * 128:(c + 1) * 128]
        return total

    def slab_copy(k, i, slot):
        other = (s + 1 + i) % n_slab
        at = s if slot is None else slot
        return pltpu.make_async_remote_copy(
            src_ref=part.at[0], dst_ref=sum_one.at[k, at],
            send_sem=send_one.at[i], recv_sem=recv_one.at[k, at],
            device_id=(b, other), device_id_type=MESH,
        )

    def bins_copy(k, i, slot):
        other = (b + 1 + i) % n_bins
        at = b if slot is None else slot
        return pltpu.make_async_remote_copy(
            src_ref=part.at[1], dst_ref=sum_two.at[k, at],
            send_sem=send_two.at[i], recv_sem=recv_two.at[k, at],
            device_id=(other, s), device_id_type=MESH,
        )

    momentum = momentum_table(ITERS)

    def iteration(k):
        change = point[...] - point_old[...]
        squares = change * change
        shift = force[...] - force_old[...]
        curve = (imb[...] * shift * shift).reshape(n_lo * 8, HI)
        part[0, 0:1, :] = lanes(squares)
        part[0, 1:2, :] = lanes(curve) + lanes(comp_ref[...] * squares)
        part[0, 2:8, :] = jnp.zeros((6, 128), F32)

        @functools.partial(loop, n_slab - 1)
        def send_slab(i):
            slab_copy(k, i, None).start()
        sum_one[k, s] = part[0]

        for l in range(n_lo):
            lead, rest = split(fvb[l, 0:6] + imb[l, 0:6] * force[l, 0:6])
            table[l * 12:l * 12 + 6, :] = lead
            table[l * 12 + 6:l * 12 + 12, :] = rest
        av[0:n_lo * 12, :] = table[0:n_lo * 12, :].astype(BF)

        @functools.partial(loop, 8)
        def pull(e):
            for c in range(halo // ck):
                at = pl.ds(c * ck, ck)
                out_v[e, 0:6, at] = gather(
                    av[0:n_lo * 12, :], halo_lo32[e, :, at], halo_hot[e, :, at], 0, n_lo
                )

            @pl.when(exists(e))
            def _():
                copy(out_v, in_v, send_v, recv_v, e).start()

        @functools.partial(loop, n_slab - 1)
        def wait_slab(i):
            slab_copy(k, i, (s + 1 + i) % n_slab).wait_recv()
        part[1] = functools.reduce(lambda x, y: x + y, [sum_one[k, i] for i in range(n_slab)])

        @functools.partial(loop, n_bins - 1)
        def send_bins(i):
            bins_copy(k, i, None).start()
        sum_two[k, b] = part[1]

        @functools.partial(loop, 2 * contacts // ck)
        def local_part(i):
            at = chunk(i, ck)
            speed[0:6, at] = gather(av[0:n_lo * 12, :], lo32[:, at], hot[:, at], 0, n_lo)

        @functools.partial(loop, n_bins - 1)
        def wait_bins(i):
            bins_copy(k, i, (b + 1 + i) % n_bins).wait_recv()
        total = functools.reduce(lambda x, y: x + y, [sum_two[k, i] for i in range(n_bins)])
        total = jnp.sum(total, axis=1, keepdims=True)
        step = (
            SAFETY * (total[0:1] / contacts_total + TINY) / (total[1:2] / contacts_total + TINY)
        )

        for e in range(8):
            @pl.when(exists(e))
            def _():
                arrival(out_v, in_v, send_v, recv_v, e).wait_recv()
            for m in range(h_lo):
                row = (n_lo + e * h_lo + m) * 12
                lead, rest = split(in_v[e, 0:6, m * HI:(m + 1) * HI])
                table[row:row + 6, :] = lead
                table[row + 6:row + 12, :] = rest
        av[n_lo * 12:, :] = table[n_lo * 12:, :].astype(BF)

        beta = jnp.float32(0.0)
        for i in range(ITERS - 1):
            beta = jnp.where(k == i, jnp.float32(momentum[i]), beta)

        @functools.partial(loop, contacts // ck)
        def update(i):
            at = chunk(i, ck)
            to = pl.ds(pl.multiple_of(contacts + i * ck, ck), ck)
            second = speed[0:6, to] + gather(
                av[n_lo * 12:, :], lo32[:, to], hot[:, to], n_lo, halo_los
            )
            first = speed[0:6, at]
            compliance = comp_ref[:, at]
            moved = []
            for r in range(3):
                here = point[r:r + 1, at]
                product = jac_ref[0, r, :, at] * first + jac_ref[1, r, :, at] * second
                slope = bias_ref[r:r + 1, at] + compliance * here + jnp.sum(product, axis=0, keepdims=True)
                moved.append(here - step * slope)
            updated = project(*moved, fric_ref[:, at])
            for r in range(3):
                point_old[r:r + 1, at] = point[r:r + 1, at]
                point[r:r + 1, at] = updated[r] + beta * (updated[r] - gamma[r:r + 1, at])
                gamma[r:r + 1, at] = updated[r]

        force_old[...] = force[...]

        @functools.partial(loop, 8)
        def sent(e):
            @pl.when(exists(e))
            def _():
                copy(out_v, in_v, send_v, recv_v, e).wait_send()

        @functools.partial(loop, n_slab - 1)
        def sent_slab(i):
            slab_copy(k, i, None).wait_send()

        @functools.partial(loop, n_bins - 1)
        def sent_bins(i):
            bins_copy(k, i, None).wait_send()

        spread()

    spread(prepare_halo)
    loop(ITERS, iteration)
    imp_ref[...] = gamma[...]
    for l in range(n_lo):
        vel_ref[:, l * HI:(l + 1) * HI] = (fvb[l] + imb[l] * force[l])[0:6]


def shards(
    n_bins, n_slab,
    free_velocity, inverse_mass, first_body, second_body, send_list,
    jacobian, contact_bias, compliance, friction, warm_start,
):
    bodies = free_velocity.shape[1]
    contacts = first_body.shape[0]
    halo = send_list.shape[1]
    n_lo = bodies // HI
    all_lo = n_lo + 8 * (halo // HI)
    dma = pltpu.SemaphoreType.DMA
    vm = pltpu.VMEM
    scratch = [
        vm((HI, 2 * contacts), BF), vm((8, 2 * contacts), jnp.int32), vm((16, 2 * contacts), BF),
        vm((8, HI, halo), BF), vm((8, 8, halo), jnp.int32), vm((8, 16, halo), BF),
        vm((n_lo, 8, HI), F32), vm((n_lo, 8, HI), F32), vm((48, 2 * contacts), BF),
        vm((n_lo * 12, HI), F32), vm(((all_lo - n_lo) * 12, HI), F32),
        vm((n_lo, 8, HI), F32), vm((n_lo, 8, HI), F32), vm((all_lo * 12, HI), F32), vm((all_lo * 12, HI), BF), vm((8, 2 * contacts), F32),
        vm((3, contacts), F32), vm((3, contacts), F32), vm((3, contacts), F32),
        vm((8, 8, halo), F32), vm((8, 8, halo), F32), vm((8, 8, halo), F32), vm((8, 8, halo), F32),
        vm((2, 8, 128), F32), vm((ITERS, n_slab, 8, 128), F32), vm((ITERS, n_bins, 8, 128), F32),
        dma((8,)), dma((8,)), dma((8,)), dma((8,)),
        dma((n_slab,)), dma((ITERS, n_slab)), dma((n_bins,)), dma((ITERS, n_bins)),
    ]
    spec = pl.BlockSpec(memory_space=pltpu.VMEM)
    return pl.pallas_call(
        functools.partial(kernel, n_bins, n_slab),
        out_shape=(
            jax.ShapeDtypeStruct((3, contacts), F32),
            jax.ShapeDtypeStruct((6, bodies), F32),
        ),
        in_specs=[spec] * 10,
        out_specs=(spec, spec),
        scratch_shapes=scratch,
        compiler_params=pltpu.CompilerParams(
            collective_id=0, has_side_effects=True, vmem_limit_bytes=48 * 1024 * 1024
        ),
    )(
        free_velocity, inverse_mass, first_body[None], second_body[None], send_list,
        jacobian, contact_bias, compliance[None], friction[None], warm_start,
    )


def solution(mesh):
    return jax.shard_map(
        functools.partial(shards, mesh.shape["bins"], mesh.shape["slab"]),
        mesh=mesh,
        in_specs=(
            P(None, ("bins", "slab")),
            P(None, ("bins", "slab")),
            P(("bins", "slab")),
            P(("bins", "slab")),
            P(None, ("bins", "slab")),
            P(None, None, None, ("bins", "slab")),
            P(None, ("bins", "slab")),
            P(("bins", "slab")),
            P(("bins", "slab")),
            P(None, ("bins", "slab")),
        ),
        out_specs=(P(None, ("bins", "slab")), P(None, ("bins", "slab"))),
        check_vma=False,
    )
```

```python
import functools
import math

import jax
import jax.numpy as jnp
from jax import lax
from jax.experimental import pallas as pl
from jax.experimental.pallas import tpu as pltpu
from jax.sharding import PartitionSpec as P

ITERS = 3
SAFETY = 0.3
TINY = 1e-06
FLOOR = 1e-20
HI = 256
BF = jnp.bfloat16
F32 = jnp.float32
MESH = pl.DeviceIdType.MESH


def momentum_table(steps_count):
    theta_now = 1.0
    momentum = []
    for iteration in range(steps_count):
        theta_next = (
            -theta_now * theta_now + theta_now * math.sqrt(theta_now * theta_now + 4.0)
        ) / 2.0
        momentum.append(theta_now * (1.0 - theta_now) / (theta_now * theta_now + theta_next))
        theta_now = theta_next
    return momentum


def project(normal, tangent_one, tangent_two, friction):
    magnitude = jnp.sqrt(tangent_one * tangent_one + tangent_two * tangent_two)
    projected = jnp.maximum(friction * magnitude + normal, 0.0) / (friction * friction + 1.0)
    inside = magnitude <= friction * normal
    normal_new = jnp.where(inside, normal, projected)
    tangent_limit = friction * normal_new
    factor = tangent_limit / jnp.maximum(jnp.maximum(magnitude, tangent_limit), FLOOR)
    return normal_new, tangent_one * factor, tangent_two * factor


def split(values):
    lead = values.astype(BF).astype(F32)
    return lead, values - lead


def pack(values):
    lead, rest = split(values)
    twice = jnp.concatenate([lead, rest, lead, rest], axis=0)
    return jnp.concatenate([twice, twice], axis=0).astype(BF)


def chunk(index, width):
    return pl.ds(pl.multiple_of(index * width, width), width)


def kernel(
    n_bins, n_slab,
    fv_ref, im_ref, first_ref, second_ref, list_ref, jac_in, bias_ref, comp_ref, fric_ref, warm_ref,
    imp_ref, vel_ref,
    jac_ref, jac_sem, hot, lo32, lo16, halo_hot, halo_lo32, halo_lo16,
    fvb, imb, x48, acc, acc_halo, force, force_old, table, av, speed,
    point, point_old, gamma,
    out_f, out_v, in_f, in_v, part, sum_one, sum_two,
    send_f, recv_f, send_v, recv_v, send_one, recv_one, send_two, recv_two,
):
    bodies = fv_ref.shape[1]
    contacts = first_ref.shape[1]
    halo = list_ref.shape[1]
    n_lo = bodies // HI
    h_lo = halo // HI
    halo_los = 8 * h_lo
    ck = 512
    wide = math.gcd(contacts, 2048)
    contacts_total = 3.0 * contacts * n_bins * n_slab
    b = lax.axis_index("bins")
    s = lax.axis_index("slab")

    def place(e):
        g = e + (e + 4) // 8
        return b + g // 3 - 1, s + g % 3 - 1

    def exists(e):
        nb, ns = place(e)
        return (nb >= 0) & (nb < n_bins) & (ns >= 0) & (ns < n_slab)

    def loop(count, body):
        def step(i, carry):
            body(i)
            return carry
        lax.fori_loop(0, count, step, 0)

    jac_copy = pltpu.make_async_copy(jac_in, jac_ref, jac_sem)
    jac_copy.start()

    in_f[...] = jnp.zeros_like(in_f)
    in_v[...] = jnp.zeros_like(in_v)

    barrier = pltpu.get_barrier_semaphore()

    @functools.partial(loop, 8)
    def greet(e):
        @pl.when(exists(e))
        def _():
            pl.semaphore_signal(barrier, inc=1, device_id=place(e), device_id_type=MESH)

    @functools.partial(loop, n_slab - 1)
    def greet_slab(i):
        pl.semaphore_signal(barrier, inc=1, device_id=(b, (s + 1 + i) % n_slab), device_id_type=MESH)

    @functools.partial(loop, n_bins - 1)
    def greet_bins(i):
        pl.semaphore_signal(barrier, inc=1, device_id=((b + 1 + i) % n_bins, s), device_id_type=MESH)

    rows = lax.broadcasted_iota(jnp.int32, (HI, ck), 0)

    def index_parts(index, hot_to, lo32_to, lo16_to):
        low = jnp.broadcast_to(index // HI, (16, ck))
        hot_to[...] = jnp.where(rows == index % HI, 1.0, 0.0).astype(BF)
        lo32_to[...] = low[:8]
        lo16_to[...] = low.astype(F32).astype(BF)

    @functools.partial(loop, contacts // ck)
    def prepare(i):
        for half, ref in enumerate((first_ref, second_ref)):
            to = pl.ds(pl.multiple_of(half * contacts + i * ck, ck), ck)
            index_parts(ref[:, chunk(i, ck)], hot.at[:, to], lo32.at[:, to], lo16.at[:, to])

    def prepare_halo():
        for e in range(8):
            for c in range(halo // ck):
                to = pl.ds(c * ck, ck)
                index_parts(
                    list_ref[e:e + 1, to],
                    halo_hot.at[e, :, to], halo_lo32.at[e, :, to], halo_lo16.at[e, :, to],
                )
        for l in range(n_lo):
            fvb[l, 0:6, :] = fv_ref[:, l * HI:(l + 1) * HI]
            imb[l, 0:6, :] = im_ref[:, l * HI:(l + 1) * HI]

    fvb[...] = jnp.zeros_like(fvb)
    imb[...] = jnp.zeros_like(imb)
    out_f[...] = jnp.zeros_like(out_f)
    out_v[...] = jnp.zeros_like(out_v)
    force[...] = jnp.zeros_like(force)
    force_old[...] = jnp.zeros_like(force_old)
    point_old[...] = jnp.zeros_like(point_old)
    point[...] = warm_ref[...]
    gamma[...] = warm_ref[...]

    jac_copy.wait()
    others = (n_slab - 1) + (n_bins - 1)
    up = jnp.where(b < n_bins - 1, 1, 0)
    down = jnp.where(b > 0, 1, 0)
    right = jnp.where(s < n_slab - 1, 1, 0)
    left = jnp.where(s > 0, 1, 0)
    pl.semaphore_wait(barrier, (1 + up + down) * (1 + left + right) - 1 + others)

    def copy(source, target, send, recv, e):
        return pltpu.make_async_remote_copy(
            src_ref=source.at[e, 0:6], dst_ref=target.at[7 - e, 0:6],
            send_sem=send.at[e], recv_sem=recv.at[7 - e],
            device_id=place(e), device_id_type=MESH,
        )

    def arrival(source, target, send, recv, e):
        return pltpu.make_async_remote_copy(
            src_ref=source.at[e, 0:6], dst_ref=target.at[e, 0:6],
            send_sem=send.at[e], recv_sem=recv.at[e],
            device_id=place(e), device_id_type=MESH,
        )

    def scatter(values, low, hot_part, first_lo, count):
        tiles = [None] * (count * 12 // 16)
        zero = jnp.zeros(low.shape, BF)
        for t in range(3):
            owner = (lax.broadcasted_iota(jnp.int32, low.shape, 0) + 16 * t) // 12
            left_over = low - owner.astype(F32).astype(BF)
            part_t = values[16 * t:16 * t + 16]
            for j in range(count // 4):
                tiles[3 * j + t] = jnp.where(left_over == jnp.array(first_lo + 4 * j, BF), part_t, zero)
        tall = jnp.concatenate(tiles, axis=0)
        return lax.dot_general(tall, hot_part, (((1,), (1,)), ((), ())), preferred_element_type=F32)

    def gather(rows_of, low, hot_part, first_lo, count):
        picked = jnp.dot(rows_of, hot_part, preferred_element_type=F32)
        sums = []
        for t in range(3):
            left_over = low - (lax.broadcasted_iota(jnp.int32, low.shape, 0) + 8 * t) // 12
            total = None
            for j in range(count // 2):
                row = (3 * j + t) * 8
                term = jnp.where(left_over == first_lo + 2 * j, picked[row:row + 8], 0.0)
                total = term if total is None else total + term
            sums.append(total)
        sums = jnp.concatenate(sums, axis=0)
        return (sums[0:6] + sums[6:12]) + (sums[12:18] + sums[18:24])

    def spread(meanwhile=None):
        @functools.partial(loop, contacts // wide)
        def terms(i):
            at = chunk(i, wide)
            for half in range(2):
                x48[:, pl.ds(pl.multiple_of(half * contacts + i * wide, wide), wide)] = pack(
                    jac_ref[half, 0, :, at] * point[0:1, at]
                    + jac_ref[half, 1, :, at] * point[1:2, at]
                    + jac_ref[half, 2, :, at] * point[2:3, at]
                )

        acc_halo[...] = jnp.zeros_like(acc_halo)

        @functools.partial(loop, contacts // wide)
        def halo_part(i):
            at = pl.ds(pl.multiple_of(contacts + i * wide, wide), wide)
            acc_halo[...] += scatter(x48[:, at], lo16[:, at], hot[:, at], n_lo, halo_los)

        for e in range(8):
            for m in range(h_lo):
                row = (e * h_lo + m) * 12
                out_f[e, 0:6, m * HI:(m + 1) * HI] = acc_halo[row:row + 6] + acc_halo[row + 6:row + 12]

        @functools.partial(loop, 8)
        def send(e):
            @pl.when(exists(e))
            def _():
                copy(out_f, in_f, send_f, recv_f, e).start()

        if meanwhile is not None:
            meanwhile()
        acc[...] = jnp.zeros_like(acc)

        @functools.partial(loop, 2 * contacts // wide)
        def local_part(i):
            at = chunk(i, wide)
            acc[...] += scatter(x48[:, at], lo16[:, at], hot[:, at], 0, n_lo)

        @functools.partial(loop, 8)
        def arrived(e):
            @pl.when(exists(e))
            def _():
                arrival(out_f, in_f, send_f, recv_f, e).wait_recv()
            for c in range(halo // ck):
                at = pl.ds(c * ck, ck)
                acc[...] += scatter(
                    pack(in_f[e, 0:6, at]), halo_lo16[e, :, at], halo_hot[e, :, at], 0, n_lo
                )

        for l in range(n_lo):
            force[l, 0:6, :] = acc[l * 12:l * 12 + 6] + acc[l * 12 + 6:l * 12 + 12]

        @functools.partial(loop, 8)
        def sent(e):
            @pl.when(exists(e))
            def _():
                copy(out_f, in_f, send_f, recv_f, e).wait_send()

    def lanes(values):
        row = jnp.sum(values, axis=0, keepdims=True)
        total = row[:, 0:128]
        for c in range(1, row.shape[1] // 128):
            total = total + row[:, c * 128:(c + 1) * 128]
        return total

    def slab_copy(k, i, slot):
        other = (s + 1 + i) % n_slab
        at = s if slot is None else slot
        return pltpu.make_async_remote_copy(
            src_ref=part.at[0], dst_ref=sum_one.at[k, at],
            send_sem=send_one.at[i], recv_sem=recv_one.at[k, at],
            device_id=(b, other), device_id_type=MESH,
        )

    def bins_copy(k, i, slot):
        other = (b + 1 + i) % n_bins
        at = b if slot is None else slot
        return pltpu.make_async_remote_copy(
            src_ref=part.at[1], dst_ref=sum_two.at[k, at],
            send_sem=send_two.at[i], recv_sem=recv_two.at[k, at],
            device_id=(other, s), device_id_type=MESH,
        )

    momentum = momentum_table(ITERS)

    def iteration(k):
        change = point[...] - point_old[...]
        squares = change * change
        shift = force[...] - force_old[...]
        curve = (imb[...] * shift * shift).reshape(n_lo * 8, HI)
        part[0, 0:1, :] = lanes(squares)
        part[0, 1:2, :] = lanes(curve) + lanes(comp_ref[...] * squares)
        part[0, 2:8, :] = jnp.zeros((6, 128), F32)

        @functools.partial(loop, n_slab - 1)
        def send_slab(i):
            slab_copy(k, i, None).start()
        sum_one[k, s] = part[0]

        for l in range(n_lo):
            lead, rest = split(fvb[l, 0:6] + imb[l, 0:6] * force[l, 0:6])
            table[l * 12:l * 12 + 6, :] = lead
            table[l * 12 + 6:l * 12 + 12, :] = rest
        av[0:n_lo * 12, :] = table[0:n_lo * 12, :].astype(BF)

        @functools.partial(loop, 8)
        def pull(e):
            for c in range(halo // ck):
                at = pl.ds(c * ck, ck)
                out_v[e, 0:6, at] = gather(
                    av[0:n_lo * 12, :], halo_lo32[e, :, at], halo_hot[e, :, at], 0, n_lo
                )

            @pl.when(exists(e))
            def _():
                copy(out_v, in_v, send_v, recv_v, e).start()

        @functools.partial(loop, n_slab - 1)
        def wait_slab(i):
            slab_copy(k, i, (s + 1 + i) % n_slab).wait_recv()
        part[1] = functools.reduce(lambda x, y: x + y, [sum_one[k, i] for i in range(n_slab)])

        @functools.partial(loop, n_bins - 1)
        def send_bins(i):
            bins_copy(k, i, None).start()
        sum_two[k, b] = part[1]

        @functools.partial(loop, 2 * contacts // wide)
        def local_part(i):
            at = chunk(i, wide)
            speed[0:6, at] = gather(av[0:n_lo * 12, :], lo32[:, at], hot[:, at], 0, n_lo)

        @functools.partial(loop, n_bins - 1)
        def wait_bins(i):
            bins_copy(k, i, (b + 1 + i) % n_bins).wait_recv()
        total = functools.reduce(lambda x, y: x + y, [sum_two[k, i] for i in range(n_bins)])
        total = jnp.sum(total, axis=1, keepdims=True)
        step = (
            SAFETY * (total[0:1] / contacts_total + TINY) / (total[1:2] / contacts_total + TINY)
        )

        for e in range(8):
            @pl.when(exists(e))
            def _():
                arrival(out_v, in_v, send_v, recv_v, e).wait_recv()
            for m in range(h_lo):
                row = (n_lo + e * h_lo + m) * 12
                lead, rest = split(in_v[e, 0:6, m * HI:(m + 1) * HI])
                table[row:row + 6, :] = lead
                table[row + 6:row + 12, :] = rest
        av[n_lo * 12:, :] = table[n_lo * 12:, :].astype(BF)

        beta = jnp.float32(0.0)
        for i in range(ITERS - 1):
            beta = jnp.where(k == i, jnp.float32(momentum[i]), beta)

        @functools.partial(loop, contacts // wide)
        def update(i):
            at = chunk(i, wide)
            to = pl.ds(pl.multiple_of(contacts + i * wide, wide), wide)
            second = speed[0:6, to] + gather(
                av[n_lo * 12:, :], lo32[:, to], hot[:, to], n_lo, halo_los
            )
            first = speed[0:6, at]
            compliance = comp_ref[:, at]
            moved = []
            for r in range(3):
                here = point[r:r + 1, at]
                product = jac_ref[0, r, :, at] * first + jac_ref[1, r, :, at] * second
                slope = bias_ref[r:r + 1, at] + compliance * here + jnp.sum(product, axis=0, keepdims=True)
                moved.append(here - step * slope)
            updated = project(*moved, fric_ref[:, at])
            for r in range(3):
                point_old[r:r + 1, at] = point[r:r + 1, at]
                point[r:r + 1, at] = updated[r] + beta * (updated[r] - gamma[r:r + 1, at])
                gamma[r:r + 1, at] = updated[r]

        force_old[...] = force[...]

        @functools.partial(loop, 8)
        def sent(e):
            @pl.when(exists(e))
            def _():
                copy(out_v, in_v, send_v, recv_v, e).wait_send()

        @functools.partial(loop, n_slab - 1)
        def sent_slab(i):
            slab_copy(k, i, None).wait_send()

        @functools.partial(loop, n_bins - 1)
        def sent_bins(i):
            bins_copy(k, i, None).wait_send()

        spread()

    spread(prepare_halo)
    loop(ITERS, iteration)
    imp_ref[...] = gamma[...]
    for l in range(n_lo):
        vel_ref[:, l * HI:(l + 1) * HI] = (fvb[l] + imb[l] * force[l])[0:6]


def shards(
    n_bins, n_slab,
    free_velocity, inverse_mass, first_body, second_body, send_list,
    jacobian, contact_bias, compliance, friction, warm_start,
):
    bodies = free_velocity.shape[1]
    contacts = first_body.shape[0]
    halo = send_list.shape[1]
    n_lo = bodies // HI
    all_lo = n_lo + 8 * (halo // HI)
    dma = pltpu.SemaphoreType.DMA
    vm = pltpu.VMEM
    scratch = [
        vm((2, 3, 6, contacts), F32), dma,
        vm((HI, 2 * contacts), BF), vm((8, 2 * contacts), jnp.int32), vm((16, 2 * contacts), BF),
        vm((8, HI, halo), BF), vm((8, 8, halo), jnp.int32), vm((8, 16, halo), BF),
        vm((n_lo, 8, HI), F32), vm((n_lo, 8, HI), F32), vm((48, 2 * contacts), BF),
        vm((n_lo * 12, HI), F32), vm(((all_lo - n_lo) * 12, HI), F32),
        vm((n_lo, 8, HI), F32), vm((n_lo, 8, HI), F32), vm((all_lo * 12, HI), F32), vm((all_lo * 12, HI), BF), vm((8, 2 * contacts), F32),
        vm((3, contacts), F32), vm((3, contacts), F32), vm((3, contacts), F32),
        vm((8, 8, halo), F32), vm((8, 8, halo), F32), vm((8, 8, halo), F32), vm((8, 8, halo), F32),
        vm((2, 8, 128), F32), vm((ITERS, n_slab, 8, 128), F32), vm((ITERS, n_bins, 8, 128), F32),
        dma((8,)), dma((8,)), dma((8,)), dma((8,)),
        dma((n_slab,)), dma((ITERS, n_slab)), dma((n_bins,)), dma((ITERS, n_bins)),
    ]
    spec = pl.BlockSpec(memory_space=pltpu.VMEM)
    return pl.pallas_call(
        functools.partial(kernel, n_bins, n_slab),
        out_shape=(
            jax.ShapeDtypeStruct((3, contacts), F32),
            jax.ShapeDtypeStruct((6, bodies), F32),
        ),
        in_specs=[spec] * 5 + [pl.BlockSpec(memory_space=pl.ANY)] + [spec] * 4,
        out_specs=(spec, spec),
        scratch_shapes=scratch,
        compiler_params=pltpu.CompilerParams(
            collective_id=0, has_side_effects=True, vmem_limit_bytes=48 * 1024 * 1024
        ),
    )(
        free_velocity, inverse_mass, first_body[None], second_body[None], send_list,
        jacobian, contact_bias, compliance[None], friction[None], warm_start,
    )


def solution(mesh):
    return jax.shard_map(
        functools.partial(shards, mesh.shape["bins"], mesh.shape["slab"]),
        mesh=mesh,
        in_specs=(
            P(None, ("bins", "slab")),
            P(None, ("bins", "slab")),
            P(("bins", "slab")),
            P(("bins", "slab")),
            P(None, ("bins", "slab")),
            P(None, None, None, ("bins", "slab")),
            P(None, ("bins", "slab")),
            P(("bins", "slab")),
            P(("bins", "slab")),
            P(None, ("bins", "slab")),
        ),
        out_specs=(P(None, ("bins", "slab")), P(None, ("bins", "slab"))),
        check_vma=False,
    )
```
